512 devices in a mesh: pipe: 8 (over x, core), dp: 64 (over y, z).
Axes of the slice: x: 4, y: 4, z: 16, core: 2. Of those that a mesh axis runs over, the one named last changes fastest.
Arguments:
- acts: bfloat16 [8, 8192, 8192], P('pipe', 'dp'), may hold values from -6 to 6
- incoming: bfloat16 [8, 8192, 8192], P('pipe', 'dp'), may hold values from -6 to 6
- proj_in: bfloat16 [64, 8192], P(None, 'dp'), may hold values from -0.0625 to 0.0625
- proj_out: bfloat16 [64, 8192], P(None, 'dp'), may hold values from -0.0625 to 0.0625
- valid_rows: bfloat16 [8, 128, 4096], P('pipe', 'dp'), may hold values from -0.09375 to 0.09375
- lengths: int32 [64], P('dp'), may hold values from 1 to 128, 7168 in all
- domains: int32 [64], replicated, may hold values from 0 to 63
Outputs:
- domain_gram: float32 [8, 64, 128, 128], P('pipe', 'dp')
The draws below stay inside these ranges and needn't reach their ends.
All inputs are finite; a program needn't handle non-finite values. No bound on the sum of `lengths` on one device may be relied on, other than what follows from the above.
Results may differ from the reference program's by a relative error of at most 0.004.
Values may be sent and summed in bfloat16 or wider, within the bound.
No kernel may reach another device: no remote copies, remote signals or barrier semaphores. Data moves between devices by JAX's collectives and lax.ppermute only.
A program may use at most 128 MiB of HBM per device.

```python
import math
import jax
import jax.numpy as jnp
import numpy as np
from jax import lax

D = 8192
K = 64
KK = 4096
Q = 128
LEN = 128
LAYERS = 8
EXAMPLES = 64
DOMAINS = 64
TOKENS = 8192


def draw_domains(key, part):
    first_key = jax.random.fold_in(key, 11)
    second_key = jax.random.fold_in(key, 12)
    label_key = jax.random.fold_in(key, 13)
    place_key = jax.random.fold_in(key, 14)
    first_pick = jax.random.randint(first_key, (EXAMPLES,), 0, DOMAINS, dtype=jnp.int32)
    second_pick = jax.random.randint(second_key, (EXAMPLES,), 0, DOMAINS, dtype=jnp.int32)
    labels = jax.random.permutation(label_key, DOMAINS).astype(jnp.int32)
    picked = labels[jnp.minimum(first_pick, second_pick)]
    first_slot = jax.random.randint(place_key, (), 0, EXAMPLES, dtype=jnp.int32)
    second_slot = (first_slot + EXAMPLES // 2) % EXAMPLES
    slots = jnp.arange(EXAMPLES, dtype=jnp.int32)
    picked = jnp.where(slots == first_slot, DOMAINS - 1, picked)
    picked = jnp.where(slots == second_slot, 0, picked)
    return picked.astype(jnp.int32)


def steps_of(rng, shape, shards, least, high):
    def one(position, blocks):
        heights = jax.random.uniform(jax.random.fold_in(jax.random.fold_in(rng, 6), position), (blocks,), jnp.float32, least / len(shards), high / len(shards))
        return jnp.repeat(jnp.exp(heights), shape[position] // blocks).reshape((-1,) + (1,) * (len(shape) - position - 1))

    loudness = one(*shards[0])
    for cut in shards[1:]:
        loudness = loudness * one(*cut)
    return loudness


def profile(amount, total, limit, slope):
    portions = [(1 << 20) // math.isqrt(rank ** slope) + 1 for rank in range(2, amount + 1)]
    surplus, given = total - limit - (amount - 1), [1] * (amount - 1)
    while surplus > 0:
        free = [i for i in range(amount - 1) if given[i] < limit]
        pool, budget = sum([portions[i] for i in free]), surplus
        for i in free:
            more = min(limit - given[i], max(1, budget * portions[i] // pool), surplus)
            given[i] = given[i] + more
            surplus = surplus - more
    return np.array([limit] + given)


def uneven(rng, count, total, reach, slope):
    if count == 2:
        one = jax.random.randint(rng, (), max(1, total - reach), min(reach, total - 1) + 1)
        return jnp.stack([one, total - one])
    tallies = jnp.asarray(profile(count, total, reach, slope), jnp.int32)
    pairs = (count - 1) // 2
    source_of, receiver = tallies[1:1 + 2 * pairs:2], tallies[2:2 + 2 * pairs:2]
    slack = jnp.minimum(source_of - 1, reach - receiver)
    passed = jax.random.randint(jax.random.fold_in(rng, 1), (pairs,), 0, 1 << 20) % (slack + 1)
    tallies = tallies.at[1:1 + 2 * pairs:2].set(source_of - passed).at[2:2 + 2 * pairs:2].set(receiver + passed)
    return tallies[jax.random.permutation(jax.random.fold_in(rng, 2), count)]


def scatter_about(stream_key, shape, width, most, split=(), held_as=jnp.bfloat16):
    loudness = steps_of(stream_key, shape, split, -0.22, 0.18) if split else 1.0
    drawn = jax.random.normal(stream_key, shape, jnp.float32) * width * loudness
    return jnp.minimum(jnp.maximum(drawn, -most), most).astype(held_as)


def setup_inputs(seed: int = 0) -> dict:
    streams_of = jax.random.split(jax.random.key(seed), 8)
    acts = scatter_about(streams_of[0], (LAYERS, TOKENS, D), 1.0, 6.0, ((0, 8), (1, 64)))
    incoming = scatter_about(streams_of[1], (LAYERS, TOKENS, D), 1.0, 6.0, ((0, 8), (1, 64)))
    proj_in = scatter_about(streams_of[2], (K, D), D ** -0.5, 0.0625, ((1, 64),))
    proj_out = scatter_about(streams_of[3], (K, D), D ** -0.5, 0.0625, ((1, 64),))
    valid_rows = scatter_about(streams_of[4], (LAYERS, Q, KK), KK ** -0.5, 0.09375, ((0, 8), (1, 64)))
    lengths = uneven(streams_of[5], EXAMPLES, 7 * EXAMPLES * LEN // 8, LEN, 0).astype(jnp.int32)
    domains = draw_domains(jax.random.fold_in(streams_of[7], 71), 0)
    return dict(acts=acts, incoming=incoming, proj_in=proj_in, proj_out=proj_out, valid_rows=valid_rows, lengths=lengths, domains=domains)


highest_precision = lax.Precision.HIGHEST


def reference(acts, incoming, proj_in, proj_out, valid_rows, lengths, domains):
    count_ex = lengths.shape[0]
    positions = jnp.arange(LEN, dtype=jnp.int32)
    live = (positions[None, :] < lengths[:, None]).astype(jnp.float32)
    weights = live / lengths[:, None].astype(jnp.float32)
    owners = (domains[:, None] == jnp.arange(DOMAINS, dtype=jnp.int32)[None, :]).astype(jnp.float32)
    out_f32 = proj_out.astype(jnp.float32)

    def per_layer(carry, layer_in):
        layer_act, branch, valid = layer_in
        grad = carry + branch.astype(jnp.float32)
        proj_act = jnp.dot(layer_act, proj_in.T, preferred_element_type=jnp.float32)
        proj_grad = jnp.dot(grad, out_f32.T, precision=highest_precision)
        scaled = proj_grad.reshape(count_ex, LEN, K) * weights[:, :, None]
        rows = jnp.einsum("eta,etb->eab", scaled, proj_act.reshape(count_ex, LEN, K), precision=highest_precision)
        rows = rows.reshape(count_ex, K * K).astype(jnp.bfloat16)
        scores = jnp.dot(rows, valid.T, preferred_element_type=jnp.float32)
        outer = jnp.einsum("eq,er->eqr", scores, scores, precision=highest_precision)
        gram = jnp.einsum("ed,eqr->dqr", owners, outer, precision=highest_precision)
        return grad, gram

    start_grad = jnp.zeros((TOKENS, D), jnp.float32)
    final_grad, grams = lax.scan(per_layer, start_grad, (acts, incoming, valid_rows), reverse=True)
    return grams
```

```python
import jax
import jax.numpy as jnp
from jax import lax
from jax.experimental import pallas as pl
from jax.experimental.pallas import tpu as pltpu
from jax.sharding import Mesh
from jax.sharding import PartitionSpec as P

HIGHEST = lax.Precision.HIGHEST
NX, NC, NY, NZ = 4, 2, 4, 16
NT = (((1,), (1,)), ((), ()))
f32, bf16 = jnp.float32, jnp.bfloat16


def spread(block, axes, count):
    sent = jnp.broadcast_to(block[None], (count,) + block.shape)
    return lax.all_to_all(sent, axes, 0, 0)


def project_kernel(w_ref, act_own, act_par, inc_own, inc_par, out_ref, acc_ref):
    step = pl.program_id(0)

    @pl.when(step == 0)
    def _():
        acc_ref[...] = jnp.zeros_like(acc_ref)

    w = jnp.concatenate(
        [w_ref[:, 0, z].reshape(NX * 16, 128) for z in range(NZ)], axis=1
    )
    act = jnp.concatenate([act_own[...], act_par[...]], axis=0)
    inc = jnp.concatenate([inc_own[...], inc_par[...]], axis=0)
    acc_ref[0] += lax.dot_general(w, act, NT, preferred_element_type=f32)
    acc_ref[1] += lax.dot_general(w, inc, NT, preferred_element_type=f32)

    @pl.when(step == NY - 1)
    def _():
        my_x, my_c = lax.axis_index("x"), lax.axis_index("c")
        own_a, par_a = acc_ref[0, :, 0:128], acc_ref[0, :, 128:256]
        own_p, par_p = acc_ref[1, :, 0:128], acc_ref[1, :, 128:256]
        both = own_p + par_p
        odd = jnp.where(my_c == 1, own_p, par_p)
        zero = jnp.zeros_like(both)
        row = lax.broadcasted_iota(jnp.int32, (64, 128), 0)
        is_act = lax.rem(lax.div(row, 8), 2) == 0
        for x in range(NX):
            for c in range(NC):
                here = x == my_x
                upper = jnp.where(x < my_x, both, zero)
                grad = jnp.where(here, both if c == 0 else odd, upper)
                act_c = jnp.where(here, jnp.where(my_c == c, own_a, par_a), zero)
                out_ref[x * NC + c] = jnp.where(is_act, act_c, grad)


def project(w, act_own, act_par, inc_own, inc_par):
    wide = act_own.shape[1] // NY
    data = pl.BlockSpec((128, wide), lambda i: (0, i))
    return pl.pallas_call(
        project_kernel,
        grid=(NY,),
        out_shape=jax.ShapeDtypeStruct((NX * NC, 64, 128), f32),
        in_specs=[pl.BlockSpec((NX, 1, NZ, 16, 128), lambda i: (0, i, 0, 0, 0))] + [data] * 4,
        out_specs=pl.BlockSpec((NX * NC, 64, 128), lambda i: (0, 0, 0)),
        scratch_shapes=[pltpu.VMEM((2, 64, 256), f32)],
        compiler_params=pltpu.CompilerParams(vmem_limit_bytes=32 * 2**20),
        cost_estimate=pl.CostEstimate(
            flops=2 * 256 * 8192 * 64 * 2, bytes_accessed=9 * 2**20, transcendentals=0
        ),
    )(w, act_own, act_par, inc_own, inc_par)


def score_kernel(len_ref, parts_ref, valid_ref, out_ref):
    live = len_ref[0]
    tok = lax.broadcasted_iota(jnp.int32, (32, 128), 1)
    weight = jnp.where(tok < live, 1.0, 0.0).astype(f32) / live.astype(f32)
    totals = []
    for c in range(NC):
        total = parts_ref[c]
        for x in range(1, NX):
            total = total + parts_ref[x * NC + c]
        totals.append(total.reshape(NX, 2, 8, 128))
    act = jnp.concatenate([t[:, 0].reshape(32, 128) for t in totals], axis=0)
    row = jnp.concatenate(
        [
            lax.dot_general(
                t[:, 1].reshape(32, 128) * weight, act, NT,
                precision=HIGHEST, preferred_element_type=f32,
            )
            for t in totals
        ],
        axis=1,
    )
    row = row.astype(bf16).astype(f32)
    part = jnp.sum(valid_ref[...].astype(f32) * row[None], axis=1)
    out_ref[...] = lax.dot_general(
        jnp.ones((64, 128), f32), part, NT, precision=HIGHEST, preferred_element_type=f32
    )


def score(lengths, parts, valid):
    vmem = pl.BlockSpec(memory_space=pltpu.VMEM)
    return pl.pallas_call(
        score_kernel,
        out_shape=jax.ShapeDtypeStruct((64, 128), f32),
        in_specs=[pl.BlockSpec(memory_space=pltpu.SMEM), vmem, vmem],
        out_specs=vmem,
        compiler_params=pltpu.CompilerParams(vmem_limit_bytes=32 * 2**20),
        cost_estimate=pl.CostEstimate(
            flops=2 * 128 * 4096, bytes_accessed=2**20, transcendentals=0
        ),
    )(lengths, parts, valid)


def body(acts, incoming, proj_in, proj_out, valid_rows, lengths, domains):
    x, c = lax.axis_index("x"), lax.axis_index("c")
    y, z = lax.axis_index("y"), lax.axis_index("z")
    swap = [(0, 1), (1, 0)]
    act_own, inc_own = acts[0], incoming[0]
    mine_in = lax.dynamic_slice(proj_in, (c * 32 + x * 8, 0), (8, 128))
    mine_out = lax.dynamic_slice(
        proj_out.reshape(32, 2, 128), (x * 8, c, 0), (8, 1, 128)
    ).reshape(8, 128)
    mine = jnp.concatenate([mine_in, mine_out], axis=0)
    along_z = spread(mine, "z", NZ)
    act_par = lax.ppermute(act_own, "c", swap)
    inc_par = lax.ppermute(inc_own, "c", swap)
    w = spread(along_z, ("x", "y"), NX * NY).reshape(NX, NY, NZ, 16, 128)
    valid = spread(spread(valid_rows.reshape(64, 128), "z", NZ), "y", NY)
    parts = lax.all_to_all(project(w, act_own, act_par, inc_own, inc_par), ("x", "c"), 0, 0)
    scores = score(lengths, parts, valid.reshape(128, 32, 128))
    scores = lax.all_to_all(scores.reshape(64, 1, 128), ("y", "z"), 0, 0).reshape(64, 128)
    owned = (domains == y * NZ + z).astype(f32)
    kept = scores * owned[:, None]
    gram = lax.dot_general(kept, scores, (((0,), (0,)), ((), ())), precision=HIGHEST)
    return gram[None, None]


def solution(mesh):
    fine = Mesh(mesh.devices.reshape(NX, NC, NY, NZ), ("x", "c", "y", "z"))
    pipe, dp = ("x", "c"), ("y", "z")
    placed = (
        P(pipe, dp, None),
        P(pipe, dp, None),
        P(None, dp),
        P(None, dp),
        P(pipe, dp, None),
        P(dp),
        P(),
    )
    return jax.shard_map(
        body, mesh=fine, in_specs=placed, out_specs=P(pipe, dp, None, None), check_vma=False
    )
```

```python
import jax
import jax.numpy as jnp
from jax import lax
from jax.experimental import pallas as pl
from jax.experimental.pallas import tpu as pltpu
from jax.sharding import Mesh
from jax.sharding import PartitionSpec as P

HIGHEST = lax.Precision.HIGHEST
NX, NC, NY, NZ = 4, 2, 4, 16
NT = (((1,), (1,)), ((), ()))
MIB = 2**20
f32, bf16 = jnp.float32, jnp.bfloat16
VMEM = pl.BlockSpec(memory_space=pltpu.VMEM)
SMEM = pl.BlockSpec(memory_space=pltpu.SMEM)


def params(mib=60):
    return pltpu.CompilerParams(vmem_limit_bytes=mib * MIB)


def cost(flops, moved):
    return pl.CostEstimate(flops=flops, bytes_accessed=moved, transcendentals=0)


def pack_kernel(in_ref, out_ref, valid_ref, sent_ref, proj_ref, rows_ref):
    x, c = lax.axis_index("x"), lax.axis_index("c")
    proj_ref[0] = in_ref[...].astype(f32)
    proj_ref[1] = out_ref[...].astype(f32)
    rows_ref[0:8] = proj_ref[0, pl.ds(c * 32 + x * 8, 8)]
    rows_ref[8:16] = proj_ref[1, pl.ds(x * 16 + c, 8, stride=2)]
    for r in range(32):
        pair = valid_ref[0, :, r * 128 : (r + 1) * 128].astype(f32)
        rows_ref[16 + r : 17 + r] = pair[0:1]
        rows_ref[48 + r : 49 + r] = pair[1:2]
    sent_ref[...] = jnp.broadcast_to(rows_ref[...].astype(bf16)[None], (NZ, 80, 128))


def pack(proj_in, proj_out, valid_rows):
    return pl.pallas_call(
        pack_kernel,
        out_shape=pltpu.HBM((NZ, 80, 128), bf16),
        in_specs=[VMEM] * 3,
        out_specs=VMEM,
        scratch_shapes=[pltpu.VMEM((2, 64, 128), f32), pltpu.VMEM((80, 128), f32)],
        compiler_params=params(32),
        cost_estimate=cost(0, 368 * 1024),
    )(*in_hbm(proj_in, proj_out, valid_rows))


def split_kernel(got_ref, proj_ref, valid_ref):
    proj_ref[...] = jnp.broadcast_to(got_ref[:, 0:16][None], (NX * NY, NZ, 16, 128))
    valid_ref[...] = got_ref[:, 16:80]


def split(got):
    return pl.pallas_call(
        split_kernel,
        out_shape=(
            pltpu.HBM((NX * NY, NZ, 16, 128), bf16),
            jax.ShapeDtypeStruct((NZ, 64, 128), bf16),
        ),
        in_specs=[VMEM],
        out_specs=(VMEM, VMEM),
        compiler_params=params(32),
        cost_estimate=cost(0, 1536 * 1024),
    )(got)


def project_half(w_ref, own_ref, par_ref, data_ref, sems):
    wide = own_ref.shape[1] // 2
    copies = []
    for half in range(2):
        for k, ref in enumerate((own_ref, par_ref)):
            copy = pltpu.make_async_copy(
                ref.at[:, pl.ds(half * wide, wide)],
                data_ref.at[pl.ds(k * 128, 128), pl.ds(half * wide, wide)],
                sems.at[half, k],
            )
            copy.start()
            copies.append(copy)
    total = None
    for half in range(2):
        w = jnp.concatenate(
            [
                w_ref[:, y, z].reshape(NX * 16, 128)
                for y in range(2 * half, 2 * half + 2)
                for z in range(NZ)
            ],
            axis=1,
        )
        copies[2 * half].wait()
        copies[2 * half + 1].wait()
        part = lax.dot_general(
            w, data_ref[:, half * wide : (half + 1) * wide], NT, preferred_element_type=f32
        )
        total = part if total is None else total + part
    return total


def half_rows(value, which):
    return value.reshape(NX, 2, 8, value.shape[1])[:, which].reshape(32, value.shape[1])


def grad_kernel(w_ref, own_ref, par_ref, out_ref, data_ref, sems):
    total = half_rows(project_half(w_ref, own_ref, par_ref, data_ref, sems), 1)
    my_x, my_c = lax.axis_index("x"), lax.axis_index("c")
    own, par = total[:, 0:128], total[:, 128:256]
    pair = own + par
    odd = jnp.where(my_c == 1, own, par)
    zero = jnp.zeros_like(pair)
    for x in range(NX):
        upper = jnp.where(x < my_x, pair, zero)
        out_ref[x * NC] = jnp.where(x == my_x, pair, upper)
        out_ref[x * NC + 1] = jnp.where(x == my_x, odd, upper)


def act_kernel(w_ref, own_ref, par_ref, mine_ref, theirs_ref, data_ref, sems):
    total = half_rows(project_half(w_ref, own_ref, par_ref, data_ref, sems), 0)
    mine_ref[...] = total[:, 0:128]
    theirs_ref[...] = total[:, 128:256]


def in_hbm(*arrays):
    return [pltpu.with_memory_space_constraint(a, pltpu.HBM) for a in arrays]


FETCH = [pltpu.VMEM((256, 8192), bf16), pltpu.SemaphoreType.DMA((2, 2))]
HBM = pl.BlockSpec(memory_space=pltpu.HBM)


def project_grads(w, own, par):
    return pl.pallas_call(
        grad_kernel,
        out_shape=pltpu.HBM((NX * NC, 32, 128), f32),
        in_specs=[VMEM, HBM, HBM],
        out_specs=VMEM,
        scratch_shapes=FETCH,
        compiler_params=params(24),
        cost_estimate=cost(2 * 256 * 8192 * 64, 5 * MIB),
    )(w, *in_hbm(own, par))


def project_acts(w, own, par):
    return pl.pallas_call(
        act_kernel,
        out_shape=(jax.ShapeDtypeStruct((32, 128), f32), pltpu.HBM((32, 128), f32)),
        in_specs=[VMEM, HBM, HBM],
        out_specs=(VMEM, VMEM),
        scratch_shapes=FETCH,
        compiler_params=params(24),
        cost_estimate=cost(2 * 256 * 8192 * 64, 5 * MIB),
    )(w, *in_hbm(own, par))


def score_kernel(len_ref, parts_ref, mine_ref, theirs_ref, *refs):
    valid_refs, out_ref = refs[:NY], refs[NY]
    my_c, my_y = lax.axis_index("c"), lax.axis_index("y")
    live = len_ref[0]
    tok = lax.broadcasted_iota(jnp.int32, (32, 128), 1)
    weight = jnp.where(tok < live, 1.0, 0.0).astype(f32) / live.astype(f32)
    mine, theirs = mine_ref[...], theirs_ref[...]
    act = jnp.concatenate(
        [jnp.where(my_c == 0, mine, theirs), jnp.where(my_c == 0, theirs, mine)], axis=0
    )
    halves = []
    for c in range(NC):
        total = parts_ref[c]
        for x in range(1, NX):
            total = total + parts_ref[x * NC + c]
        halves.append(
            lax.dot_general(
                total * weight, act, NT, precision=HIGHEST, preferred_element_type=f32
            )
        )
    row = jnp.concatenate(halves, axis=1).astype(bf16).astype(f32)
    for k, valid_ref in enumerate(valid_refs):
        part = jnp.sum(valid_ref[...].astype(f32) * row[None], axis=1)
        scores = lax.dot_general(
            jnp.ones((64, 128), f32), part, NT, precision=HIGHEST, preferred_element_type=f32
        )
        place = lax.rem(my_y - k + NY, NY)
        for y in range(NY):

            @pl.when(place == y)
            def _():
                out_ref[:, y * 32 : (y + 1) * 32] = scores


def score(lengths, parts, mine, theirs, valid):
    return pl.pallas_call(
        score_kernel,
        out_shape=pltpu.HBM((64, 128), f32),
        in_specs=[SMEM] + [VMEM] * (3 + NY),
        out_specs=VMEM,
        compiler_params=params(32),
        cost_estimate=cost(2 * 128 * 4096, MIB),
    )(lengths, parts, mine, theirs, *valid)


def gram_kernel(dom_ref, scores_ref, out_ref):
    me = lax.axis_index("y") * NZ + lax.axis_index("z")
    scores = scores_ref[...]
    owned = jnp.where(dom_ref[...] == me, 1.0, 0.0).astype(f32)
    out_ref[...] = jnp.dot(
        scores.T * owned, scores, precision=HIGHEST, preferred_element_type=f32
    )


def gram(domains, scores):
    return pl.pallas_call(
        gram_kernel,
        out_shape=jax.ShapeDtypeStruct((128, 128), f32),
        in_specs=[VMEM, VMEM],
        out_specs=VMEM,
        compiler_params=params(24),
        cost_estimate=cost(2 * 128 * 128 * 64 * 6, 96 * 1024),
    )(domains, scores)


def body(acts, incoming, proj_in, proj_out, valid_rows, lengths, domains):
    swap = [(0, 1), (1, 0)]
    act_own, inc_own = acts[0], incoming[0]
    got = lax.all_to_all(pack(proj_in, proj_out, valid_rows), "z", 0, 0)
    inc_par = lax.ppermute(inc_own, "c", swap)
    act_par = lax.ppermute(act_own, "c", swap)
    sent, valid_here = split(got)
    w = lax.all_to_all(sent, ("x", "y"), 0, 0).reshape(NX, NY, NZ, 16, 128)
    valid = [valid_here] + [
        lax.ppermute(valid_here, "y", [(i, (i + k) % NY) for i in range(NY)]) for k in range(1, NY)
    ]
    parts = lax.all_to_all(project_grads(w, inc_own, inc_par), ("x", "c"), 0, 0)
    mine, others = project_acts(w, act_own, act_par)
    theirs = lax.ppermute(others, "c", swap)
    scores = score(lengths, parts, mine, theirs, [v.reshape(32, 32, 128) for v in valid])
    scores = lax.all_to_all(scores.reshape(64, 1, 128), ("y", "z"), 0, 0).reshape(64, 128)
    return gram(domains.reshape(1, 64), scores)[None, None]


def solution(mesh):
    fine = Mesh(mesh.devices.reshape(NX, NC, NY, NZ), ("x", "c", "y", "z"))
    pipe, dp = ("x", "c"), ("y", "z")
    placed = (
        P(pipe, dp, None),
        P(pipe, dp, None),
        P(None, dp),
        P(None, dp),
        P(pipe, dp, None),
        P(dp),
        P(),
    )
    return jax.shard_map(
        body, mesh=fine, in_specs=placed, out_specs=P(pipe, dp, None, None), check_vma=False
    )
```

```python
import jax
import jax.numpy as jnp
from jax import lax
from jax.experimental import pallas as pl
from jax.experimental.pallas import tpu as pltpu
from jax.sharding import Mesh
from jax.sharding import PartitionSpec as P

HIGHEST = lax.Precision.HIGHEST
AXES = ("x", "c", "y", "u", "p")
SIZES = NX, NC, NY, NU, NP = 4, 2, 4, 8, 2
NT = (((1,), (1,)), ((), ()))
MIB = 2**20
f32, bf16 = jnp.float32, jnp.bfloat16
VMEM = pl.BlockSpec(memory_space=pltpu.VMEM)
SMEM = pl.BlockSpec(memory_space=pltpu.SMEM)
HBM = pl.BlockSpec(memory_space=pltpu.HBM)


def in_hbm(*arrays):
    return [pltpu.with_memory_space_constraint(a, pltpu.HBM) for a in arrays]


def params(mib):
    return pltpu.CompilerParams(vmem_limit_bytes=mib * MIB)


def cost(flops, moved):
    return pl.CostEstimate(flops=flops, bytes_accessed=moved, transcendentals=0)


def pack_kernel(in_ref, out_ref, valid_ref, sent_ref, proj_ref, rows_ref):
    c = lax.axis_index("c")
    proj_ref[0] = in_ref[...].astype(f32)
    proj_ref[1] = out_ref[...].astype(f32)
    rows_ref[0:32] = proj_ref[0, pl.ds(pl.multiple_of(c * 32, 32), 32)]
    rows_ref[32:64] = proj_ref[1, pl.ds(c, 32, stride=2)]
    for r in range(32):
        pair = valid_ref[0, :, r * 128 : (r + 1) * 128].astype(f32)
        rows_ref[64 + r : 65 + r] = pair[0:1]
        rows_ref[96 + r : 97 + r] = pair[1:2]
    sent_ref[...] = jnp.broadcast_to(rows_ref[...].astype(bf16)[None], (NU, 128, 128))


def pack(proj_in, proj_out, valid_rows):
    return pl.pallas_call(
        pack_kernel,
        out_shape=pltpu.HBM((NU, 128, 128), bf16),
        in_specs=[VMEM] * 3,
        out_specs=VMEM,
        scratch_shapes=[pltpu.VMEM((2, 64, 128), f32), pltpu.VMEM((128, 128), f32)],
        compiler_params=params(32),
        cost_estimate=cost(0, 304 * 1024),
    )(*in_hbm(proj_in, proj_out, valid_rows))


def split_kernel(got_ref, proj_ref, valid_ref):
    proj_ref[...] = jnp.broadcast_to(got_ref[:, 0:64][None], (NY * NP, NU, 64, 128))
    valid_ref[...] = got_ref[:, 64:128]


def split(got):
    return pl.pallas_call(
        split_kernel,
        out_shape=(
            pltpu.HBM((NY * NP, NU, 64, 128), bf16),
            jax.ShapeDtypeStruct((NU, 64, 128), bf16),
        ),
        in_specs=[VMEM],
        out_specs=(VMEM, VMEM),
        compiler_params=params(32),
        cost_estimate=cost(0, 1536 * 1024),
    )(got)


def merge_kernel(*refs):
    for k in range(NY):
        refs[NY][k] = refs[k][...]


def merge(parts):
    return pl.pallas_call(
        merge_kernel,
        out_shape=jax.ShapeDtypeStruct((NY, NU, 64, 128), bf16),
        in_specs=[VMEM] * NY,
        out_specs=VMEM,
        compiler_params=params(32),
        cost_estimate=cost(0, MIB),
    )(*parts)


def project_half(which, w_ref, own_ref, par_ref, data_ref, sems):
    wide = own_ref.shape[1] // 2
    copies = []
    for half in range(2):
        for k, ref in enumerate((own_ref, par_ref)):
            copy = pltpu.make_async_copy(
                ref.at[:, pl.ds(half * wide, wide)],
                data_ref.at[pl.ds(k * 128, 128), pl.ds(half * wide, wide)],
                sems.at[half, k],
            )
            copy.start()
            copies.append(copy)
    total = None
    for half in range(2):
        w = jnp.concatenate(
            [
                w_ref[y, p, u, which * 32 : which * 32 + 32]
                for y in range(2 * half, 2 * half + 2)
                for u in range(NU)
                for p in range(NP)
            ],
            axis=1,
        )
        copies[2 * half].wait()
        copies[2 * half + 1].wait()
        part = lax.dot_general(
            w, data_ref[:, half * wide : (half + 1) * wide], NT, preferred_element_type=f32
        )
        total = part if total is None else total + part
    return total[:, 0:128], total[:, 128:256]


def grad_kernel(w_ref, own_ref, par_ref, out_ref, data_ref, sems):
    own, par = project_half(1, w_ref, own_ref, par_ref, data_ref, sems)
    my_x, my_c = lax.axis_index("x"), lax.axis_index("c")
    pair = own + par
    odd = jnp.where(my_c == 1, own, par)
    zero = jnp.zeros_like(pair)
    for x in range(NX):
        upper = jnp.where(x < my_x, pair, zero)
        out_ref[x * NC] = jnp.where(x == my_x, pair, upper)
        out_ref[x * NC + 1] = jnp.where(x == my_x, odd, upper)


def act_kernel(w_ref, own_ref, par_ref, mine_ref, theirs_ref, data_ref, sems):
    mine_ref[...], theirs_ref[...] = project_half(0, w_ref, own_ref, par_ref, data_ref, sems)


FETCH = [pltpu.VMEM((256, 8192), bf16), pltpu.SemaphoreType.DMA((2, 2))]


def project_grads(w, own, par):
    return pl.pallas_call(
        grad_kernel,
        out_shape=pltpu.HBM((NX * NC, 32, 128), f32),
        in_specs=[VMEM, HBM, HBM],
        out_specs=VMEM,
        scratch_shapes=FETCH,
        compiler_params=params(24),
        cost_estimate=cost(2 * 256 * 8192 * 64, 5 * MIB),
    )(w, *in_hbm(own, par))


def project_acts(w, own, par):
    return pl.pallas_call(
        act_kernel,
        out_shape=(jax.ShapeDtypeStruct((32, 128), f32), pltpu.HBM((32, 128), f32)),
        in_specs=[VMEM, HBM, HBM],
        out_specs=(VMEM, VMEM),
        scratch_shapes=FETCH,
        compiler_params=params(24),
        cost_estimate=cost(2 * 256 * 8192 * 64, 5 * MIB),
    )(w, *in_hbm(own, par))


def score_kernel(len_ref, parts_ref, mine_ref, theirs_ref, here_ref, there_ref, out_ref):
    my_c, my_y, my_p = lax.axis_index("c"), lax.axis_index("y"), lax.axis_index("p")
    live = len_ref[0]
    tok = lax.broadcasted_iota(jnp.int32, (32, 128), 1)
    weight = jnp.where(tok < live, 1.0, 0.0).astype(f32) / live.astype(f32)
    mine, theirs = mine_ref[...], theirs_ref[...]
    act = jnp.concatenate(
        [jnp.where(my_c == 0, mine, theirs), jnp.where(my_c == 0, theirs, mine)], axis=0
    )
    halves = []
    for c in range(NC):
        total = parts_ref[c]
        for x in range(1, NX):
            total = total + parts_ref[x * NC + c]
        halves.append(
            lax.dot_general(
                total * weight, act, NT, precision=HIGHEST, preferred_element_type=f32
            )
        )
    row = jnp.concatenate(halves, axis=1).astype(bf16).astype(f32)
    part = jnp.concatenate(
        [
            jnp.sum(ref[...].reshape(64, 32, 128).astype(f32) * row[None], axis=1)
            for ref in (here_ref, there_ref)
        ],
        axis=0,
    )
    came = lax.broadcasted_iota(jnp.int32, (128, 128), 0)
    y = (my_y + 4 - ((came >> 4) & 3)) & 3
    p = (my_p + (came >> 6)) & 1
    goes = y * 32 + ((came >> 1) & 7) * 4 + p * 2 + (came & 1)
    order = jnp.where(goes == lax.broadcasted_iota(jnp.int32, (128, 128), 1), 1.0, 0.0)
    scores = lax.dot_general(
        jnp.ones((64, 128), f32), part, NT, precision=HIGHEST, preferred_element_type=f32
    )
    out_ref[...] = jnp.dot(
        scores, order.astype(f32), precision=HIGHEST, preferred_element_type=f32
    )


def score(lengths, parts, mine, theirs, here, there):
    return pl.pallas_call(
        score_kernel,
        out_shape=pltpu.HBM((64, 128), f32),
        in_specs=[SMEM] + [VMEM] * 5,
        out_specs=VMEM,
        compiler_params=params(32),
        cost_estimate=cost(2 * 128 * 4096, MIB),
    )(lengths, parts, mine, theirs, here, there)


def gram_kernel(dom_ref, scores_ref, out_ref):
    me = lax.axis_index("y") * (NU * NP) + lax.axis_index("u") * NP + lax.axis_index("p")
    scores = scores_ref[...]
    owned = jnp.where(dom_ref[...] == me, 1.0, 0.0).astype(f32)
    out_ref[...] = jnp.dot(
        scores.T * owned, scores, precision=HIGHEST, preferred_element_type=f32
    )


def gram(domains, scores):
    return pl.pallas_call(
        gram_kernel,
        out_shape=jax.ShapeDtypeStruct((128, 128), f32),
        in_specs=[VMEM, VMEM],
        out_specs=VMEM,
        compiler_params=params(24),
        cost_estimate=cost(2 * 128 * 128 * 64 * 6, 96 * 1024),
    )(domains, scores)


def body(acts, incoming, proj_in, proj_out, valid_rows, lengths, domains):
    swap = [(0, 1), (1, 0)]
    act_own, inc_own = acts[0], incoming[0]
    got = lax.all_to_all(pack(proj_in, proj_out, valid_rows), "u", 0, 0)
    inc_par = lax.ppermute(inc_own, "c", swap)
    act_par = lax.ppermute(act_own, "c", swap)
    sent, valid = split(got)
    w = lax.all_to_all(sent, ("y", "p"), 0, 0).reshape(NY, NP, NU, 64, 128)
    came = [valid] + [
        lax.ppermute(valid, "y", [(i, (i + k) % NY) for i in range(NY)]) for k in range(1, NY)
    ]
    sums = project_grads(w, inc_own, inc_par)
    sums, came = lax.optimization_barrier((sums, came))
    parts = lax.all_to_all(sums, ("x", "c"), 0, 0)
    here = merge(came)
    there = lax.ppermute(here, "p", swap)
    mine, others = project_acts(w, act_own, act_par)
    theirs = lax.ppermute(others, "c", swap)
    scores = score(lengths, parts, mine, theirs, here, there)
    scores = lax.all_to_all(scores.reshape(64, 1, 128), ("y", "u", "p"), 0, 0).reshape(64, 128)
    return gram(domains.reshape(1, 64), scores)[None, None]


def solution(mesh):
    fine = Mesh(mesh.devices.reshape(SIZES), AXES)
    pipe, dp = AXES[:2], AXES[2:]
    placed = (
        P(pipe, dp, None),
        P(pipe, dp, None),
        P(None, dp),
        P(None, dp),
        P(pipe, dp, None),
        P(dp),
        P(),
    )
    return jax.shard_map(
        body, mesh=fine, in_specs=placed, out_specs=P(pipe, dp, None, None), check_vma=False
    )
```

```python
import jax
import jax.numpy as jnp
from jax import lax
from jax.experimental import pallas as pl
from jax.experimental.pallas import tpu as pltpu
from jax.sharding import Mesh
from jax.sharding import PartitionSpec as P

HIGHEST = lax.Precision.HIGHEST
AXES = ("x", "c", "y", "u", "p")
SIZES = NX, NC, NY, NU, NP = 4, 2, 4, 8, 2
NT = (((1,), (1,)), ((), ()))
MIB = 2**20
f32, bf16 = jnp.float32, jnp.bfloat16
VMEM = pl.BlockSpec(memory_space=pltpu.VMEM)
SMEM = pl.BlockSpec(memory_space=pltpu.SMEM)
HBM = pl.BlockSpec(memory_space=pltpu.HBM)


def in_hbm(*arrays):
    return [pltpu.with_memory_space_constraint(a, pltpu.HBM) for a in arrays]


def params(mib):
    return pltpu.CompilerParams(vmem_limit_bytes=mib * MIB)


def cost(flops, moved):
    return pl.CostEstimate(flops=flops, bytes_accessed=moved, transcendentals=0)


def pack_kernel(in_ref, out_ref, valid_ref, sent_ref, proj_ref, rows_ref):
    x, c = lax.axis_index("x"), lax.axis_index("c")
    proj_ref[0] = in_ref[...].astype(f32)
    proj_ref[1] = out_ref[...].astype(f32)
    rows_ref[0:8] = proj_ref[0, pl.ds(c * 32 + x * 8, 8)]
    rows_ref[8:16] = proj_ref[1, pl.ds(x * 16 + c, 8, stride=2)]
    for r in range(32):
        pair = valid_ref[0, :, r * 128 : (r + 1) * 128].astype(f32)
        rows_ref[16 + r : 17 + r] = pair[0:1]
        rows_ref[48 + r : 49 + r] = pair[1:2]
    sent_ref[...] = jnp.broadcast_to(rows_ref[...].astype(bf16)[None], (NU, 80, 128))


def pack(proj_in, proj_out, valid_rows):
    return pl.pallas_call(
        pack_kernel,
        out_shape=pltpu.HBM((NU, 80, 128), bf16),
        in_specs=[VMEM] * 3,
        out_specs=VMEM,
        scratch_shapes=[pltpu.VMEM((2, 64, 128), f32), pltpu.VMEM((80, 128), f32)],
        compiler_params=params(32),
        cost_estimate=cost(0, 208 * 1024),
    )(*in_hbm(proj_in, proj_out, valid_rows))


def split_kernel(got_ref, proj_ref, valid_ref):
    proj_ref[...] = jnp.broadcast_to(got_ref[:, 0:16][None], (NX * NY * NP, NU, 16, 128))
    valid_ref[...] = got_ref[:, 16:80]


def split(got):
    return pl.pallas_call(
        split_kernel,
        out_shape=(
            pltpu.HBM((NX * NY * NP, NU, 16, 128), bf16),
            jax.ShapeDtypeStruct((NU, 64, 128), bf16),
        ),
        in_specs=[VMEM],
        out_specs=(VMEM, VMEM),
        compiler_params=params(32),
        cost_estimate=cost(0, 1536 * 1024),
    )(got)


def merge_kernel(*refs):
    for k in range(NY):
        refs[NY][k] = refs[k][...]


def merge(parts):
    return pl.pallas_call(
        merge_kernel,
        out_shape=jax.ShapeDtypeStruct((NY, NU, 64, 128), bf16),
        in_specs=[VMEM] * NY,
        out_specs=VMEM,
        compiler_params=params(32),
        cost_estimate=cost(0, MIB),
    )(*parts)


def project_half(which, w_ref, own_ref, par_ref, data_ref, sems):
    wide = own_ref.shape[1] // 2
    copies = []
    for half in range(2):
        for k, ref in enumerate((own_ref, par_ref)):
            copy = pltpu.make_async_copy(
                ref.at[:, pl.ds(half * wide, wide)],
                data_ref.at[pl.ds(k * 128, 128), pl.ds(half * wide, wide)],
                sems.at[half, k],
            )
            copy.start()
            copies.append(copy)
    total = None
    for half in range(2):
        w = jnp.concatenate(
            [
                w_ref[:, y, p, u].reshape(NX * 16, 128)
                for y in range(2 * half, 2 * half + 2)
                for u in range(NU)
                for p in range(NP)
            ],
            axis=1,
        )
        copies[2 * half].wait()
        copies[2 * half + 1].wait()
        part = lax.dot_general(
            w, data_ref[:, half * wide : (half + 1) * wide], NT, preferred_element_type=f32
        )
        total = part if total is None else total + part
    total = total.reshape(NX, 2, 8, 256)[:, which].reshape(32, 256)
    return total[:, 0:128], total[:, 128:256]


def grad_kernel(w_ref, own_ref, par_ref, out_ref, data_ref, sems):
    own, par = project_half(1, w_ref, own_ref, par_ref, data_ref, sems)
    my_x, my_c = lax.axis_index("x"), lax.axis_index("c")
    pair = own + par
    odd = jnp.where(my_c == 1, own, par)
    zero = jnp.zeros_like(pair)
    for x in range(NX):
        upper = jnp.where(x < my_x, pair, zero)
        out_ref[x * NC] = jnp.where(x == my_x, pair, upper)
        out_ref[x * NC + 1] = jnp.where(x == my_x, odd, upper)


def act_kernel(w_ref, own_ref, par_ref, mine_ref, theirs_ref, data_ref, sems):
    mine_ref[...], theirs_ref[...] = project_half(0, w_ref, own_ref, par_ref, data_ref, sems)


FETCH = [pltpu.VMEM((256, 8192), bf16), pltpu.SemaphoreType.DMA((2, 2))]


def project_grads(w, own, par):
    return pl.pallas_call(
        grad_kernel,
        out_shape=pltpu.HBM((NX * NC, 32, 128), f32),
        in_specs=[VMEM, HBM, HBM],
        out_specs=VMEM,
        scratch_shapes=FETCH,
        compiler_params=params(24),
        cost_estimate=cost(2 * 256 * 8192 * 64, 5 * MIB),
    )(w, *in_hbm(own, par))


def project_acts(w, own, par):
    return pl.pallas_call(
        act_kernel,
        out_shape=(jax.ShapeDtypeStruct((32, 128), f32), pltpu.HBM((32, 128), f32)),
        in_specs=[VMEM, HBM, HBM],
        out_specs=(VMEM, VMEM),
        scratch_shapes=FETCH,
        compiler_params=params(24),
        cost_estimate=cost(2 * 256 * 8192 * 64, 5 * MIB),
    )(w, *in_hbm(own, par))


def score_kernel(len_ref, parts_ref, mine_ref, theirs_ref, here_ref, there_ref, out_ref):
    my_c, my_y, my_p = lax.axis_index("c"), lax.axis_index("y"), lax.axis_index("p")
    live = len_ref[0]
    tok = lax.broadcasted_iota(jnp.int32, (32, 128), 1)
    weight = jnp.where(tok < live, 1.0, 0.0).astype(f32) / live.astype(f32)
    mine, theirs = mine_ref[...], theirs_ref[...]
    act = jnp.concatenate(
        [jnp.where(my_c == 0, mine, theirs), jnp.where(my_c == 0, theirs, mine)], axis=0
    )
    halves = []
    for c in range(NC):
        total = parts_ref[c]
        for x in range(1, NX):
            total = total + parts_ref[x * NC + c]
        halves.append(
            lax.dot_general(
                total * weight, act, NT, precision=HIGHEST, preferred_element_type=f32
            )
        )
    row = jnp.concatenate(halves, axis=1).astype(bf16).astype(f32)
    part = jnp.concatenate(
        [
            jnp.sum(ref[...].reshape(64, 32, 128).astype(f32) * row[None], axis=1)
            for ref in (here_ref, there_ref)
        ],
        axis=0,
    )
    came = lax.broadcasted_iota(jnp.int32, (128, 128), 0)
    y = (my_y + 4 - ((came >> 4) & 3)) & 3
    p = (my_p + (came >> 6)) & 1
    goes = y * 32 + ((came >> 1) & 7) * 4 + p * 2 + (came & 1)
    order = jnp.where(goes == lax.broadcasted_iota(jnp.int32, (128, 128), 1), 1.0, 0.0)
    scores = lax.dot_general(
        jnp.ones((64, 128), f32), part, NT, precision=HIGHEST, preferred_element_type=f32
    )
    out_ref[...] = jnp.dot(
        scores, order.astype(f32), precision=HIGHEST, preferred_element_type=f32
    )


def score(lengths, parts, mine, theirs, here, there):
    return pl.pallas_call(
        score_kernel,
        out_shape=pltpu.HBM((64, 128), f32),
        in_specs=[SMEM] + [VMEM] * 5,
        out_specs=VMEM,
        compiler_params=params(32),
        cost_estimate=cost(2 * 128 * 4096, MIB),
    )(lengths, parts, mine, theirs, here, there)


def gram_kernel(dom_ref, scores_ref, out_ref):
    me = lax.axis_index("y") * (NU * NP) + lax.axis_index("u") * NP + lax.axis_index("p")
    scores = scores_ref[...]
    owned = jnp.where(dom_ref[...] == me, 1.0, 0.0).astype(f32)
    out_ref[...] = jnp.dot(
        scores.T * owned, scores, precision=HIGHEST, preferred_element_type=f32
    )


def gram(domains, scores):
    return pl.pallas_call(
        gram_kernel,
        out_shape=jax.ShapeDtypeStruct((128, 128), f32),
        in_specs=[VMEM, VMEM],
        out_specs=VMEM,
        compiler_params=params(24),
        cost_estimate=cost(2 * 128 * 128 * 64 * 6, 96 * 1024),
    )(domains, scores)


def body(acts, incoming, proj_in, proj_out, valid_rows, lengths, domains):
    swap = [(0, 1), (1, 0)]
    act_own, inc_own = acts[0], incoming[0]
    got = lax.all_to_all(pack(proj_in, proj_out, valid_rows), "u", 0, 0)
    inc_par = lax.ppermute(inc_own, "c", swap)
    act_par = lax.ppermute(act_own, "c", swap)
    sent, valid = split(got)
    w = lax.all_to_all(sent, ("x", "y", "p"), 0, 0).reshape(NX, NY, NP, NU, 16, 128)
    came = [valid] + [
        lax.ppermute(valid, "y", [(i, (i + k) % NY) for i in range(NY)]) for k in range(1, NY)
    ]
    sums = project_grads(w, inc_own, inc_par)
    sums, came = lax.optimization_barrier((sums, came))
    parts = lax.all_to_all(sums, ("x", "c"), 0, 0)
    here = merge(came)
    there = lax.ppermute(here, "p", swap)
    mine, others = project_acts(w, act_own, act_par)
    theirs = lax.ppermute(others, "c", swap)
    scores = score(lengths, parts, mine, theirs, here, there)
    scores = lax.all_to_all(scores.reshape(64, 1, 128), ("y", "u", "p"), 0, 0).reshape(64, 128)
    return gram(domains.reshape(1, 64), scores)[None, None]


def solution(mesh):
    fine = Mesh(mesh.devices.reshape(SIZES), AXES)
    pipe, dp = AXES[:2], AXES[2:]
    placed = (
        P(pipe, dp, None),
        P(pipe, dp, None),
        P(None, dp),
        P(None, dp),
        P(pipe, dp, None),
        P(dp),
        P(),
    )
    return jax.shard_map(
        body, mesh=fine, in_specs=placed, out_specs=P(pipe, dp, None, None), check_vma=False
    )
```

```python
import jax
import jax.numpy as jnp
from jax import lax
from jax.experimental import pallas as pl
from jax.experimental.pallas import tpu as pltpu
from jax.sharding import Mesh
from jax.sharding import PartitionSpec as P

HIGHEST = lax.Precision.HIGHEST
AXES = ("x", "c", "y", "u", "p")
SIZES = NX, NC, NY, NU, NP = 4, 2, 4, 8, 2
NT = (((1,), (1,)), ((), ()))
MIB = 2**20
f32, bf16 = jnp.float32, jnp.bfloat16
VMEM = pl.BlockSpec(memory_space=pltpu.VMEM)
SMEM = pl.BlockSpec(memory_space=pltpu.SMEM)
HBM = pl.BlockSpec(memory_space=pltpu.HBM)


def in_hbm(*arrays):
    return [pltpu.with_memory_space_constraint(a, pltpu.HBM) for a in arrays]


def params(mib):
    return pltpu.CompilerParams(vmem_limit_bytes=mib * MIB)


def cost(flops, moved):
    return pl.CostEstimate(flops=flops, bytes_accessed=moved, transcendentals=0)


def pack_kernel(in_ref, out_ref, valid_ref, sent_ref, proj_ref, rows_ref):
    x, c = lax.axis_index("x"), lax.axis_index("c")
    proj_ref[0] = in_ref[...].astype(f32)
    proj_ref[1] = out_ref[...].astype(f32)
    rows_ref[0:8] = proj_ref[0, pl.ds(c * 32 + x * 8, 8)]
    rows_ref[8:16] = proj_ref[1, pl.ds(x * 16 + c, 8, stride=2)]
    for r in range(32):
        pair = valid_ref[0, :, r * 128 : (r + 1) * 128].astype(f32)
        rows_ref[16 + r : 17 + r] = pair[0:1]
        rows_ref[48 + r : 49 + r] = pair[1:2]
    sent_ref[...] = jnp.broadcast_to(rows_ref[...].astype(bf16)[None], (NU, 80, 128))


def pack(proj_in, proj_out, valid_rows):
    return pl.pallas_call(
        pack_kernel,
        out_shape=pltpu.HBM((NU, 80, 128), bf16),
        in_specs=[VMEM] * 3,
        out_specs=VMEM,
        scratch_shapes=[pltpu.VMEM((2, 64, 128), f32), pltpu.VMEM((80, 128), f32)],
        compiler_params=params(32),
        cost_estimate=cost(0, 208 * 1024),
    )(*in_hbm(proj_in, proj_out, valid_rows))


def stack_kernel(inc_ref, act_ref, both_ref, done_ref, data_ref, in_sems, out_sems):
    arrive, leave = [], []
    for j, ref in enumerate((inc_ref, act_ref)):
        for k in range(2):
            here, row = pl.ds(k * 64, 64), pl.ds(j * 128 + k * 64, 64)
            arrive.append(
                pltpu.make_async_copy(ref.at[here], data_ref.at[row], in_sems.at[j, k])
            )
            leave.append(
                pltpu.make_async_copy(data_ref.at[row], both_ref.at[row], out_sems.at[j, k])
            )
    for copy in arrive:
        copy.start()
    done_ref[...] = jnp.zeros_like(done_ref)
    for first, second in zip(arrive, leave):
        first.wait()
        second.start()
    for copy in leave:
        copy.wait()


def stack(inc, act):
    return pl.pallas_call(
        stack_kernel,
        out_shape=(pltpu.HBM((256, 8192), bf16), jax.ShapeDtypeStruct((8, 128), f32)),
        in_specs=[HBM, HBM],
        out_specs=(HBM, VMEM),
        scratch_shapes=[
            pltpu.VMEM((256, 8192), bf16),
            pltpu.SemaphoreType.DMA((2, 2)),
            pltpu.SemaphoreType.DMA((2, 2)),
        ],
        compiler_params=params(24),
        cost_estimate=cost(0, 8 * MIB),
    )(*in_hbm(inc, act))


def split_kernel(got_ref, stacked_ref, proj_ref, valid_ref):
    proj_ref[...] = jnp.broadcast_to(got_ref[:, 0:16][None], (NX * NY * NP, NU, 16, 128))
    valid_ref[...] = got_ref[:, 16:80]


def split(got, stacked):
    return pl.pallas_call(
        split_kernel,
        out_shape=(
            pltpu.HBM((NX * NY * NP, NU, 16, 128), bf16),
            jax.ShapeDtypeStruct((NU, 64, 128), bf16),
        ),
        in_specs=[VMEM, VMEM],
        out_specs=(VMEM, VMEM),
        compiler_params=params(32),
        cost_estimate=cost(0, 1536 * 1024),
    )(got, stacked)


def merge_kernel(*refs):
    for k in range(NY):
        refs[NY][k] = refs[k][...]


def merge(parts):
    return pl.pallas_call(
        merge_kernel,
        out_shape=jax.ShapeDtypeStruct((NY, NU, 64, 128), bf16),
        in_specs=[VMEM] * NY,
        out_specs=VMEM,
        compiler_params=params(32),
        cost_estimate=cost(0, MIB),
    )(*parts)


def project_half(which, w_ref, own_ref, par_ref, data_ref, sems):
    wide = own_ref.shape[1] // 2
    copies = []
    for half in range(2):
        for k, ref in enumerate((own_ref, par_ref)):
            first = 0 if k == 0 or which == 1 else 128
            copy = pltpu.make_async_copy(
                ref.at[pl.ds(first, 128), pl.ds(half * wide, wide)],
                data_ref.at[pl.ds(k * 128, 128), pl.ds(half * wide, wide)],
                sems.at[half, k],
            )
            copy.start()
            copies.append(copy)
    total = None
    for half in range(2):
        w = jnp.concatenate(
            [
                w_ref[:, y, p, u].reshape(NX * 16, 128)
                for y in range(2 * half, 2 * half + 2)
                for u in range(NU)
                for p in range(NP)
            ],
            axis=1,
        )
        copies[2 * half].wait()
        copies[2 * half + 1].wait()
        part = lax.dot_general(
            w, data_ref[:, half * wide : (half + 1) * wide], NT, preferred_element_type=f32
        )
        total = part if total is None else total + part
    total = total.reshape(NX, 2, 8, 256)[:, which].reshape(32, 256)
    return total[:, 0:128], total[:, 128:256]


def grad_kernel(w_ref, own_ref, par_ref, out_ref, data_ref, sems):
    own, par = project_half(1, w_ref, own_ref, par_ref, data_ref, sems)
    my_x, my_c = lax.axis_index("x"), lax.axis_index("c")
    pair = own + par
    odd = jnp.where(my_c == 1, own, par)
    zero = jnp.zeros_like(pair)
    for x in range(NX):
        upper = jnp.where(x < my_x, pair, zero)
        out_ref[x * NC] = jnp.where(x == my_x, pair, upper)
        out_ref[x * NC + 1] = jnp.where(x == my_x, odd, upper)


def act_kernel(w_ref, own_ref, par_ref, mine_ref, theirs_ref, data_ref, sems):
    mine_ref[...], theirs_ref[...] = project_half(0, w_ref, own_ref, par_ref, data_ref, sems)


FETCH = [pltpu.VMEM((256, 8192), bf16), pltpu.SemaphoreType.DMA((2, 2))]


def project_grads(w, own, par):
    return pl.pallas_call(
        grad_kernel,
        out_shape=pltpu.HBM((NX * NC, 32, 128), f32),
        in_specs=[VMEM, HBM, HBM],
        out_specs=VMEM,
        scratch_shapes=FETCH,
        compiler_params=params(24),
        cost_estimate=cost(2 * 256 * 8192 * 64, 5 * MIB),
    )(w, *in_hbm(own, par))


def project_acts(w, own, par):
    return pl.pallas_call(
        act_kernel,
        out_shape=(jax.ShapeDtypeStruct((32, 128), f32), pltpu.HBM((32, 128), f32)),
        in_specs=[VMEM, HBM, HBM],
        out_specs=(VMEM, VMEM),
        scratch_shapes=FETCH,
        compiler_params=params(24),
        cost_estimate=cost(2 * 256 * 8192 * 64, 5 * MIB),
    )(w, *in_hbm(own, par))


def score_kernel(len_ref, parts_ref, mine_ref, theirs_ref, here_ref, there_ref, out_ref):
    my_c, my_y, my_p = lax.axis_index("c"), lax.axis_index("y"), lax.axis_index("p")
    live = len_ref[0]
    tok = lax.broadcasted_iota(jnp.int32, (32, 128), 1)
    weight = jnp.where(tok < live, 1.0, 0.0).astype(f32) / live.astype(f32)
    mine, theirs = mine_ref[...], theirs_ref[...]
    act = jnp.concatenate(
        [jnp.where(my_c == 0, mine, theirs), jnp.where(my_c == 0, theirs, mine)], axis=0
    )
    halves = []
    for c in range(NC):
        total = parts_ref[c]
        for x in range(1, NX):
            total = total + parts_ref[x * NC + c]
        halves.append(
            lax.dot_general(
                total * weight, act, NT, precision=HIGHEST, preferred_element_type=f32
            )
        )
    row = jnp.concatenate(halves, axis=1).astype(bf16).astype(f32)
    part = jnp.concatenate(
        [
            jnp.sum(ref[...].reshape(64, 32, 128).astype(f32) * row[None], axis=1)
            for ref in (here_ref, there_ref)
        ],
        axis=0,
    )
    came = lax.broadcasted_iota(jnp.int32, (128, 128), 0)
    y = (my_y + 4 - ((came >> 4) & 3)) & 3
    p = (my_p + (came >> 6)) & 1
    goes = y * 32 + ((came >> 1) & 7) * 4 + p * 2 + (came & 1)
    order = jnp.where(goes == lax.broadcasted_iota(jnp.int32, (128, 128), 1), 1.0, 0.0)
    scores = lax.dot_general(
        jnp.ones((64, 128), f32), part, NT, precision=HIGHEST, preferred_element_type=f32
    )
    out_ref[...] = jnp.dot(
        scores, order.astype(f32), precision=HIGHEST, preferred_element_type=f32
    )


def score(lengths, parts, mine, theirs, here, there):
    return pl.pallas_call(
        score_kernel,
        out_shape=pltpu.HBM((64, 128), f32),
        in_specs=[SMEM] + [VMEM] * 5,
        out_specs=VMEM,
        compiler_params=params(32),
        cost_estimate=cost(2 * 128 * 4096, MIB),
    )(lengths, parts, mine, theirs, here, there)


def gram_kernel(dom_ref, scores_ref, out_ref):
    me = lax.axis_index("y") * (NU * NP) + lax.axis_index("u") * NP + lax.axis_index("p")
    scores = scores_ref[...]
    owned = jnp.where(dom_ref[...] == me, 1.0, 0.0).astype(f32)
    out_ref[...] = jnp.dot(
        scores.T * owned, scores, precision=HIGHEST, preferred_element_type=f32
    )


def gram(domains, scores):
    return pl.pallas_call(
        gram_kernel,
        out_shape=jax.ShapeDtypeStruct((128, 128), f32),
        in_specs=[VMEM, VMEM],
        out_specs=VMEM,
        compiler_params=params(24),
        cost_estimate=cost(2 * 128 * 128 * 64 * 6, 96 * 1024),
    )(domains, scores)


def body(acts, incoming, proj_in, proj_out, valid_rows, lengths, domains):
    swap = [(0, 1), (1, 0)]
    act_own, inc_own = acts[0], incoming[0]
    got = lax.all_to_all(pack(proj_in, proj_out, valid_rows), "u", 0, 0)
    both, stacked = stack(inc_own, act_own)
    par = lax.ppermute(both, "c", swap)
    sent, valid = split(got, stacked)
    w = lax.all_to_all(sent, ("x", "y", "p"), 0, 0).reshape(NX, NY, NP, NU, 16, 128)
    came = [valid] + [
        lax.ppermute(valid, "y", [(i, (i + k) % NY) for i in range(NY)]) for k in range(1, NY)
    ]
    sums = project_grads(w, inc_own, par)
    sums, came = lax.optimization_barrier((sums, came))
    parts = lax.all_to_all(sums, ("x", "c"), 0, 0)
    here = merge(came)
    there = lax.ppermute(here, "p", swap)
    mine, others = project_acts(w, act_own, par)
    theirs = lax.ppermute(others, "c", swap)
    scores = score(lengths, parts, mine, theirs, here, there)
    scores = lax.all_to_all(scores.reshape(64, 1, 128), ("y", "u", "p"), 0, 0).reshape(64, 128)
    return gram(domains.reshape(1, 64), scores)[None, None]


def solution(mesh):
    fine = Mesh(mesh.devices.reshape(SIZES), AXES)
    pipe, dp = AXES[:2], AXES[2:]
    placed = (
        P(pipe, dp, None),
        P(pipe, dp, None),
        P(None, dp),
        P(None, dp),
        P(pipe, dp, None),
        P(dp),
        P(),
    )
    return jax.shard_map(
        body, mesh=fine, in_specs=placed, out_specs=P(pipe, dp, None, None), check_vma=False
    )
```

```python
import jax
import jax.numpy as jnp
from jax import lax
from jax.experimental import pallas as pl
from jax.experimental.pallas import tpu as pltpu
from jax.sharding import Mesh
from jax.sharding import PartitionSpec as P

HIGHEST = lax.Precision.HIGHEST
AXES = ("x", "c", "y", "u", "p")
SIZES = NX, NC, NY, NU, NP = 4, 2, 4, 8, 2
NT = (((1,), (1,)), ((), ()))
MIB = 2**20
f32, bf16 = jnp.float32, jnp.bfloat16
VMEM = pl.BlockSpec(memory_space=pltpu.VMEM)
SMEM = pl.BlockSpec(memory_space=pltpu.SMEM)
HBM = pl.BlockSpec(memory_space=pltpu.HBM)


def in_hbm(*arrays):
    return [pltpu.with_memory_space_constraint(a, pltpu.HBM) for a in arrays]


def params(mib):
    return pltpu.CompilerParams(vmem_limit_bytes=mib * MIB)


def cost(flops, moved):
    return pl.CostEstimate(flops=flops, bytes_accessed=moved, transcendentals=0)


def pack_kernel(in_ref, out_ref, valid_ref, sent_ref, proj_ref, rows_ref):
    x, c = lax.axis_index("x"), lax.axis_index("c")
    proj_ref[0] = in_ref[...].astype(f32)
    proj_ref[1] = out_ref[...].astype(f32)
    rows_ref[0:8] = proj_ref[0, pl.ds(c * 32 + x * 8, 8)]
    rows_ref[8:16] = proj_ref[1, pl.ds(x * 16 + c, 8, stride=2)]
    for r in range(32):
        pair = valid_ref[0, :, r * 128 : (r + 1) * 128].astype(f32)
        rows_ref[16 + r : 17 + r] = pair[0:1]
        rows_ref[48 + r : 49 + r] = pair[1:2]
    sent_ref[...] = jnp.broadcast_to(rows_ref[...].astype(bf16)[None], (NU, 80, 128))


def pack(proj_in, proj_out, valid_rows):
    return pl.pallas_call(
        pack_kernel,
        out_shape=pltpu.HBM((NU, 80, 128), bf16),
        in_specs=[VMEM] * 3,
        out_specs=VMEM,
        scratch_shapes=[pltpu.VMEM((2, 64, 128), f32), pltpu.VMEM((80, 128), f32)],
        compiler_params=params(32),
        cost_estimate=cost(0, 208 * 1024),
    )(*in_hbm(proj_in, proj_out, valid_rows))


def stack_kernel(inc_ref, act_ref, both_ref, order_ref, data_ref, in_sems, out_sems):
    arrive, leave = [], []
    for j, ref in enumerate((inc_ref, act_ref)):
        for k in range(2):
            here, row = pl.ds(k * 64, 64), pl.ds(j * 128 + k * 64, 64)
            arrive.append(
                pltpu.make_async_copy(ref.at[here], data_ref.at[row], in_sems.at[j, k])
            )
            leave.append(
                pltpu.make_async_copy(data_ref.at[row], both_ref.at[row], out_sems.at[j, k])
            )
    for copy in arrive:
        copy.start()
    my_y, my_p = lax.axis_index("y"), lax.axis_index("p")
    came = lax.broadcasted_iota(jnp.int32, (128, 128), 0)
    y = (my_y + 4 - ((came >> 4) & 3)) & 3
    p = (my_p + (came >> 6)) & 1
    goes = y * 32 + ((came >> 1) & 7) * 4 + p * 2 + (came & 1)
    order = jnp.where(goes == lax.broadcasted_iota(jnp.int32, (128, 128), 1), 1.0, 0.0)
    order_ref[...] = order.astype(f32)
    for first, second in zip(arrive, leave):
        first.wait()
        second.start()
    for copy in leave:
        copy.wait()


def stack(inc, act):
    return pl.pallas_call(
        stack_kernel,
        out_shape=(pltpu.HBM((256, 8192), bf16), jax.ShapeDtypeStruct((128, 128), f32)),
        in_specs=[HBM, HBM],
        out_specs=(HBM, VMEM),
        scratch_shapes=[
            pltpu.VMEM((256, 8192), bf16),
            pltpu.SemaphoreType.DMA((2, 2)),
            pltpu.SemaphoreType.DMA((2, 2)),
        ],
        compiler_params=params(24),
        cost_estimate=cost(0, 8 * MIB),
    )(*in_hbm(inc, act))


def split_kernel(got_ref, order_ref, proj_ref, valid_ref):
    proj_ref[...] = jnp.broadcast_to(got_ref[:, 0:16][None], (NX * NY * NP, NU, 16, 128))
    valid_ref[...] = got_ref[:, 16:80]


def split(got, order):
    return pl.pallas_call(
        split_kernel,
        out_shape=(
            pltpu.HBM((NX * NY * NP, NU, 16, 128), bf16),
            jax.ShapeDtypeStruct((NU, 64, 128), bf16),
        ),
        in_specs=[VMEM, VMEM],
        out_specs=(VMEM, VMEM),
        compiler_params=params(32),
        cost_estimate=cost(0, 1536 * 1024),
    )(got, order)


def merge_kernel(*refs):
    for k in range(NY):
        refs[NY][k] = refs[k][...]


def merge(parts):
    return pl.pallas_call(
        merge_kernel,
        out_shape=jax.ShapeDtypeStruct((NY, NU, 64, 128), bf16),
        in_specs=[VMEM] * NY,
        out_specs=VMEM,
        compiler_params=params(32),
        cost_estimate=cost(0, MIB),
    )(*parts)


def project_half(which, w_ref, own_ref, par_ref, data_ref, sems):
    wide = own_ref.shape[1] // 2
    copies = []
    for half in range(2):
        for k, ref in enumerate((own_ref, par_ref)):
            first = 0 if k == 0 or which == 1 else 128
            copy = pltpu.make_async_copy(
                ref.at[pl.ds(first, 128), pl.ds(half * wide, wide)],
                data_ref.at[pl.ds(k * 128, 128), pl.ds(half * wide, wide)],
                sems.at[half, k],
            )
            copy.start()
            copies.append(copy)
    total = None
    for half in range(2):
        w = jnp.concatenate(
            [
                w_ref[p, :, y, u].reshape(NX * 16, 128)
                for y in range(2 * half, 2 * half + 2)
                for u in range(NU)
                for p in range(NP)
            ],
            axis=1,
        )
        copies[2 * half].wait()
        copies[2 * half + 1].wait()
        part = lax.dot_general(
            w, data_ref[:, half * wide : (half + 1) * wide], NT, preferred_element_type=f32
        )
        total = part if total is None else total + part
    total = total.reshape(NX, 2, 8, 256)[:, which].reshape(32, 256)
    return total[:, 0:128], total[:, 128:256]


def grad_kernel(w_ref, own_ref, par_ref, out_ref, data_ref, sems):
    own, par = project_half(1, w_ref, own_ref, par_ref, data_ref, sems)
    my_x, my_c = lax.axis_index("x"), lax.axis_index("c")
    pair = own + par
    odd = jnp.where(my_c == 1, own, par)
    zero = jnp.zeros_like(pair)
    for x in range(NX):
        upper = jnp.where(x < my_x, pair, zero)
        out_ref[x * NC] = jnp.where(x == my_x, pair, upper)
        out_ref[x * NC + 1] = jnp.where(x == my_x, odd, upper)


def act_kernel(w_ref, own_ref, par_ref, mine_ref, theirs_ref, data_ref, sems):
    mine_ref[...], theirs_ref[...] = project_half(0, w_ref, own_ref, par_ref, data_ref, sems)


FETCH = [pltpu.VMEM((256, 8192), bf16), pltpu.SemaphoreType.DMA((2, 2))]


def project_grads(w, own, par):
    return pl.pallas_call(
        grad_kernel,
        out_shape=pltpu.HBM((NX * NC, 32, 128), f32),
        in_specs=[VMEM, HBM, HBM],
        out_specs=VMEM,
        scratch_shapes=FETCH,
        compiler_params=params(24),
        cost_estimate=cost(2 * 256 * 8192 * 64, 5 * MIB),
    )(w, *in_hbm(own, par))


def project_acts(w, own, par):
    return pl.pallas_call(
        act_kernel,
        out_shape=(jax.ShapeDtypeStruct((32, 128), f32), pltpu.HBM((32, 128), f32)),
        in_specs=[VMEM, HBM, HBM],
        out_specs=(VMEM, VMEM),
        scratch_shapes=FETCH,
        compiler_params=params(24),
        cost_estimate=cost(2 * 256 * 8192 * 64, 5 * MIB),
    )(w, *in_hbm(own, par))


def score_kernel(len_ref, order_ref, parts_ref, mine_ref, theirs_ref, here_ref, there_ref, out_ref):
    my_c = lax.axis_index("c")
    live = len_ref[0]
    tok = lax.broadcasted_iota(jnp.int32, (32, 128), 1)
    weight = jnp.where(tok < live, 1.0, 0.0).astype(f32) / live.astype(f32)
    mine, theirs = mine_ref[...], theirs_ref[...]
    act = jnp.concatenate(
        [jnp.where(my_c == 0, mine, theirs), jnp.where(my_c == 0, theirs, mine)], axis=0
    )
    halves = []
    for c in range(NC):
        total = parts_ref[c]
        for x in range(1, NX):
            total = total + parts_ref[x * NC + c]
        halves.append(
            lax.dot_general(
                total * weight, act, NT, precision=HIGHEST, preferred_element_type=f32
            )
        )
    row = jnp.concatenate(halves, axis=1).astype(bf16).astype(f32)
    part = jnp.concatenate(
        [
            jnp.sum(ref[...].reshape(64, 32, 128).astype(f32) * row[None], axis=1)
            for ref in (here_ref, there_ref)
        ],
        axis=0,
    )
    scores = lax.dot_general(
        jnp.ones((8, 128), f32), part, NT, precision=HIGHEST, preferred_element_type=f32
    )
    scores = jnp.dot(scores, order_ref[...], precision=HIGHEST, preferred_element_type=f32)
    out_ref[...] = jnp.concatenate([scores] * 8, axis=0)


def score(lengths, order, parts, mine, theirs, here, there):
    return pl.pallas_call(
        score_kernel,
        out_shape=pltpu.HBM((64, 128), f32),
        in_specs=[SMEM] + [VMEM] * 6,
        out_specs=VMEM,
        compiler_params=params(32),
        cost_estimate=cost(2 * 128 * 4096, MIB),
    )(lengths, order, parts, mine, theirs, here, there)


def gram_kernel(dom_ref, scores_ref, out_ref):
    me = lax.axis_index("y") * (NU * NP) + lax.axis_index("u") * NP + lax.axis_index("p")
    scores = scores_ref[...]
    owned = jnp.where(dom_ref[...] == me, 1.0, 0.0).astype(f32)
    out_ref[...] = jnp.dot(
        scores.T * owned, scores, precision=HIGHEST, preferred_element_type=f32
    )


def gram(domains, scores):
    return pl.pallas_call(
        gram_kernel,
        out_shape=jax.ShapeDtypeStruct((128, 128), f32),
        in_specs=[VMEM, VMEM],
        out_specs=VMEM,
        compiler_params=params(24),
        cost_estimate=cost(2 * 128 * 128 * 64 * 6, 96 * 1024),
    )(domains, scores)


def body(acts, incoming, proj_in, proj_out, valid_rows, lengths, domains):
    swap = [(0, 1), (1, 0)]
    act_own, inc_own = acts[0], incoming[0]
    got = lax.all_to_all(pack(proj_in, proj_out, valid_rows), "u", 0, 0)
    both, order = stack(inc_own, act_own)
    par = lax.ppermute(both, "c", swap)
    sent, valid = split(got, order)
    w = lax.all_to_all(sent, ("p", "x", "y"), 0, 0).reshape(NP, NX, NY, NU, 16, 128)
    came = [valid] + [
        lax.ppermute(valid, "y", [(i, (i + k) % NY) for i in range(NY)]) for k in range(1, NY)
    ]
    sums = project_grads(w, inc_own, par)
    sums, came = lax.optimization_barrier((sums, came))
    parts = lax.all_to_all(sums, ("x", "c"), 0, 0)
    here = merge(came)
    there = lax.ppermute(here, "p", swap)
    mine, others = project_acts(w, act_own, par)
    theirs = lax.ppermute(others, "c", swap)
    scores = score(lengths, order, parts, mine, theirs, here, there)
    scores = lax.all_to_all(scores.reshape(64, 1, 128), ("y", "u", "p"), 0, 0).reshape(64, 128)
    return gram(domains.reshape(1, 64), scores)[None, None]


def solution(mesh):
    fine = Mesh(mesh.devices.reshape(SIZES), AXES)
    pipe, dp = AXES[:2], AXES[2:]
    placed = (
        P(pipe, dp, None),
        P(pipe, dp, None),
        P(None, dp),
        P(None, dp),
        P(pipe, dp, None),
        P(dp),
        P(),
    )
    return jax.shard_map(
        body, mesh=fine, in_specs=placed, out_specs=P(pipe, dp, None, None), check_vma=False
    )
```
